256 devices in a mesh: section: 64 (over x, y, z_hi, core), tp: 4 (over z_lo).
Axes of the slice: x: 4, y: 4, z: 8 (z_hi: 2, z_lo: 4; z = z_hi * 4 + z_lo), core: 2. Of those that a mesh axis runs over, the one named last changes fastest.
Arguments:
- queries: bfloat16 [24576, 6144], P('section', 'tp'), may hold values from -60 to 60
- keys: bfloat16 [24576, 6144], P('section', 'tp'), may hold values from -6 to 6
- values: bfloat16 [24576, 6144], P('section', 'tp'), may hold values from -40 to 40
- cotangent: bfloat16 [24576, 6144], P('section', 'tp'), may hold values from -6 to 6
- doc_ids: int32 [24576], P('section'), may hold values from 0 to 15, never falling along the last dimension, each value on 1 to 3072 neighbouring positions
- gain: float32 [6144], P('tp'), may hold values from 0.1 to 1.9
Outputs:
- normed: bfloat16 [24576, 6144], P('section', 'tp')
- grad_queries: bfloat16 [24576, 6144], P('section', 'tp')
- grad_keys: bfloat16 [24576, 6144], P('section', 'tp')
- grad_values: bfloat16 [24576, 6144], P('section', 'tp')
The draws below stay inside these ranges and needn't reach their ends.
All inputs are finite; a program needn't handle non-finite values.
Results may differ from the reference program's by a relative error of at most 0.009.
Values may be sent and summed in bfloat16 or wider, within the bound.
No kernel may reach another device: no remote copies, remote signals or barrier semaphores. Data moves between devices by JAX's collectives and lax.ppermute only.
A program may use at most 192 MiB of HBM per device.

```python
import math
import jax
import jax.numpy as jnp
import numpy as np
from jax import lax

HS = 128
TOK_DEV = 384
BAND_DEV = 2
HEADS = 48
F = 6144
SEQ = 24576
WIN = 768
DOCS = 16
DOC_MOST = 3072
N_SECTION = 64


def draw_queries(key, part):
    key = jax.random.fold_in(key, 11)
    first_key = jax.random.fold_in(key, 0)
    drawn = jnp.clip(jax.random.normal(first_key, (SEQ, F), jnp.float32), -6.0, 6.0)
    return drawn.astype(jnp.bfloat16)


def draw_keys(key, part):
    key = jax.random.fold_in(key, 23)
    drawn = jnp.clip(jax.random.normal(key, (SEQ, F), jnp.float32), -6.0, 6.0)
    return drawn.astype(jnp.bfloat16)


def draw_values(key, part):
    key = jax.random.fold_in(key, 37)
    first_key, second_key = jax.random.split(key)
    column_ramp = jnp.arange(F, dtype=jnp.float32) / max(F - 1, 1)
    base_part = jnp.clip(jax.random.normal(first_key, (SEQ, F), jnp.float32), -6.0, 6.0)
    column_scale = jnp.exp(column_ramp * jnp.log(3.0)) / jnp.sqrt(3.0)
    row_scale = jnp.exp(jax.random.uniform(second_key, (SEQ, 1), jnp.float32, jnp.log(0.32), jnp.log(3.2)))
    drawn = base_part * column_scale[None, :] * row_scale
    return drawn.astype(jnp.bfloat16)


def levels(stream_key, extent, cuts, low, top_value):
    def one(position, shards_of):
        steps = jax.random.uniform(jax.random.fold_in(jax.random.fold_in(stream_key, 6), position), (shards_of,), jnp.float32, low / len(cuts), top_value / len(cuts))
        return jnp.repeat(jnp.exp(steps), extent[position] // shards_of).reshape((-1,) + (1,) * (len(extent) - position - 1))

    factor_of = one(*cuts[0])
    for cut in cuts[1:]:
        factor_of = factor_of * one(*cut)
    return factor_of


def split_up(count, total, most, lean):
    weights = [(1 << 20) // math.isqrt(rank ** lean) + 1 for rank in range(2, count + 1)]
    spare, given = total - most - (count - 1), [1] * (count - 1)
    while spare > 0:
        movable = [i for i in range(count - 1) if given[i] < most]
        pool, left = sum([weights[i] for i in movable]), spare
        for i in movable:
            addition = min(most - given[i], max(1, left * weights[i] // pool), spare)
            given[i] = given[i] + addition
            spare = spare - addition
    return np.array([most] + given)


def uneven_parts(stream_key, number_of, total, most, skew):
    if number_of == 2:
        one = jax.random.randint(stream_key, (), max(1, total - most), min(most, total - 1) + 1)
        return jnp.stack([one, total - one])
    lengths = jnp.asarray(split_up(number_of, total, most, skew), jnp.int32)
    couples = (number_of - 1) // 2
    donor, sink = lengths[1:1 + 2 * couples:2], lengths[2:2 + 2 * couples:2]
    slack = jnp.minimum(donor - 1, most - sink)
    shifted = jax.random.randint(jax.random.fold_in(stream_key, 1), (couples,), 0, 1 << 20) % (slack + 1)
    lengths = lengths.at[1:1 + 2 * couples:2].set(donor - shifted).at[2:2 + 2 * couples:2].set(sink + shifted)
    return lengths[jax.random.permutation(jax.random.fold_in(stream_key, 2), number_of)]


def gaussian(rng, extent, width, bound, cuts=(), kind=jnp.bfloat16):
    result = jax.random.normal(rng, extent, jnp.float32) * width
    if len(cuts) > 0:
        result = levels(rng, extent, cuts, -0.22, 0.18) * result
    return jnp.clip(result, min=-bound, max=bound).astype(kind)


def setup_inputs(seed: int = 0) -> dict:
    key_list = jax.random.split(jax.random.key(seed), 7)
    queries = draw_queries(jax.random.fold_in(key_list[6], 71), 0)
    keys = draw_keys(jax.random.fold_in(key_list[6], 71), 0)
    values = draw_values(jax.random.fold_in(key_list[6], 71), 0)
    cotangent = gaussian(key_list[3], (SEQ, F), 1.0, 6.0, ((0, 64), (1, 4)))
    doc_ids = jnp.searchsorted(jnp.cumsum(uneven_parts(key_list[4], DOCS, SEQ, DOC_MOST, 0)), jnp.arange(SEQ), side="right").astype(jnp.int32)
    gain = jnp.clip(1.0 + 0.18 * jax.random.normal(key_list[5], (F,), jnp.float32), 0.1, 1.9)
    return {"queries": queries, "keys": keys, "values": values, "cotangent": cotangent, "doc_ids": doc_ids, "gain": gain}


def band_mask(query_pos, query_doc, key_pos, key_doc, window):
    distance = query_pos[:, None] - key_pos[None, :]
    return (distance >= 0) & (distance < window) & (key_pos[None, :] >= 0) & (query_doc[:, None] == key_doc[None, :])

def reference(queries, keys, values, cotangent, doc_ids, gain):
    margin = BAND_DEV * TOK_DEV
    span = (BAND_DEV + 1) * TOK_DEV
    score_scale = HS ** (-0.5)
    key_pad = jnp.concatenate([jnp.zeros((margin, F), keys.dtype), keys], 0)
    value_pad = jnp.concatenate([jnp.zeros((margin, F), values.dtype), values], 0)
    doc_pad = jnp.concatenate([-jnp.ones((margin,), jnp.int32), doc_ids], 0)
    offsets = jnp.arange(TOK_DEV, dtype=jnp.int32)
    band_offsets = jnp.arange(span, dtype=jnp.int32)

    def gather_band(block):
        start = (block * TOK_DEV).astype(jnp.int32)
        query_block = lax.dynamic_slice_in_dim(queries, start, TOK_DEV, 0).reshape(TOK_DEV, HEADS, HS).astype(jnp.float32)
        key_band = lax.dynamic_slice_in_dim(key_pad, start, span, 0).reshape(span, HEADS, HS).astype(jnp.float32)
        value_band = lax.dynamic_slice_in_dim(value_pad, start, span, 0).reshape(span, HEADS, HS).astype(jnp.float32)
        query_doc = lax.dynamic_slice_in_dim(doc_ids, start, TOK_DEV, 0)
        key_doc = lax.dynamic_slice_in_dim(doc_pad, start, span, 0)
        visible = band_mask(start + offsets, query_doc, start - margin + band_offsets, key_doc, WIN)
        scores = jnp.einsum('qhd,khd->hqk', query_block, key_band) * score_scale
        scores = jnp.where(visible[None], scores, -1e+30)
        return (start, query_block, key_band, value_band, scores)

    def forward(block):
        start, query_block, key_band, value_band, scores = gather_band(block)
        row_max = lax.optimization_barrier(jnp.max(scores, axis=-1, keepdims=True))
        log_total = row_max + jnp.log(lax.optimization_barrier(jnp.sum(jnp.exp(scores - row_max), axis=-1, keepdims=True)))
        weights_b = jnp.exp(scores - log_total).astype(jnp.bfloat16).astype(jnp.float32)
        attended = jnp.einsum('hqk,khd->qhd', weights_b, value_band)
        return (attended.reshape(TOK_DEV, F), log_total[:, :, 0])
    blocks = jnp.arange(N_SECTION, dtype=jnp.int32)
    attended, log_totals = lax.map(forward, blocks)
    attended = attended.reshape(SEQ, F)
    inverse = lax.rsqrt(lax.optimization_barrier(jnp.sum(attended * attended, axis=-1, keepdims=True)) / F + 1e-05)
    normed = (attended * inverse * gain).astype(jnp.bfloat16)
    scaled_grad = cotangent.astype(jnp.float32) * gain
    inner_sum = lax.optimization_barrier(jnp.sum(scaled_grad * attended, axis=-1, keepdims=True))
    grad_out = (inverse * scaled_grad - attended * inverse ** 3 * inner_sum / F).astype(jnp.bfloat16)
    row_delta = lax.optimization_barrier(jnp.sum(grad_out.astype(jnp.float32).reshape(SEQ, HEADS, HS) * attended.reshape(SEQ, HEADS, HS), axis=-1))

    def backward(carry, block):
        grad_key_pad, grad_value_pad = carry
        start, query_block, key_band, value_band, scores = gather_band(block)
        log_block = lax.dynamic_index_in_dim(log_totals, block, 0, keepdims=False)
        weights = jnp.exp(scores - log_block[:, :, None])
        weights_b = weights.astype(jnp.bfloat16).astype(jnp.float32)
        grad_block = lax.dynamic_slice_in_dim(grad_out, start, TOK_DEV, 0).reshape(TOK_DEV, HEADS, HS).astype(jnp.float32)
        delta_block = lax.dynamic_slice_in_dim(row_delta, start, TOK_DEV, 0).T
        grad_weights = jnp.einsum('qhd,khd->hqk', grad_block, value_band)
        dscore = (weights * (grad_weights - delta_block[:, :, None])).astype(jnp.bfloat16).astype(jnp.float32)
        grad_query = jnp.einsum('hqk,khd->qhd', dscore, key_band) * score_scale
        key_part = (jnp.einsum('hqk,qhd->khd', dscore, query_block) * score_scale).reshape(span, F)
        value_part = jnp.einsum('hqk,qhd->khd', weights_b, grad_block).reshape(span, F)
        grad_key_pad = lax.dynamic_update_slice_in_dim(grad_key_pad, lax.dynamic_slice_in_dim(grad_key_pad, start, span, 0) + key_part, start, 0)
        grad_value_pad = lax.dynamic_update_slice_in_dim(grad_value_pad, lax.dynamic_slice_in_dim(grad_value_pad, start, span, 0) + value_part, start, 0)
        return ((grad_key_pad, grad_value_pad), grad_query.reshape(TOK_DEV, F))
    empty = jnp.zeros((SEQ + margin, F), jnp.float32)
    (grad_key_pad, grad_value_pad), grad_queries = lax.scan(backward, (empty, empty), blocks)
    grad_queries = grad_queries.reshape(SEQ, F).astype(jnp.bfloat16)
    grad_keys = grad_key_pad[margin:].astype(jnp.bfloat16)
    grad_values = grad_value_pad[margin:].astype(jnp.bfloat16)
    return (normed, grad_queries, grad_keys, grad_values)
```

```python
import functools
import math

import jax
import jax.numpy as jnp
from jax import lax
from jax.experimental import pallas as pl
from jax.experimental.pallas import tpu as pltpu
from jax.sharding import PartitionSpec as P

HS = 128
SCALE = HS**-0.5
SCALE2 = SCALE * math.log2(math.e)
HIDDEN = -1e30
CHUNKS = (6, 6)
HANDED = ((0, 3), (3, 6), (6, 12))
STATS = 32
F32 = jnp.float32
BF16 = jnp.bfloat16


def send(value, pairs):
    return lax.ppermute(value, "section", pairs)


def after(value, *earlier):
    return lax.optimization_barrier((value, *earlier))[0]


def dot_nt(a, b):
    return lax.dot_general(a, b, (((1,), (1,)), ((), ())), preferred_element_type=F32)


def dot_nn(a, b):
    return lax.dot_general(a, b, (((1,), (0,)), ((), ())), preferred_element_type=F32)


def as_columns(row):
    return jnp.broadcast_to(row, (128, row.shape[1])).T


def write_bias(bias, key_rows, query_rows, kinds):
    for b, (key_row, query_row, kind) in enumerate(zip(key_rows, query_rows, kinds)):
        n = key_row.shape[1]
        key_doc = jnp.concatenate([as_columns(key_row)] * (n // 128), axis=1)
        visible = key_doc == query_row
        key_pos = lax.broadcasted_iota(jnp.int32, (n, n), 0)
        query_pos = lax.broadcasted_iota(jnp.int32, (n, n), 1)
        if kind == "own":
            visible = visible & (key_pos <= query_pos)
        elif kind == "far":
            visible = visible & (key_pos > query_pos)
        bias[b] = jnp.where(visible, 0.0, HIDDEN)


def choose(core_ref, scratch, for_core0, for_core1):
    @pl.when(core_ref[0] == 0)
    def _():
        scratch[...] = for_core0[...]

    @pl.when(core_ref[0] != 0)
    def _():
        scratch[...] = for_core1[...]


def forward_kernel(
    core_ref, d0, d1, d2, q, k0, kc, kd, k2, v0, vc, vd, v2, cot, gain,
    o, lse, stat, bias, k1, v1, squares, inner,
):
    h = pl.program_id(0)

    @pl.when(h == 0)
    def _():
        rows = [d[0:1, :] for d in (d0, d1, d2)]
        write_bias(bias, rows, [rows[0]] * 3, ("own", "near", "far"))
        squares[...] = jnp.zeros_like(squares)
        inner[...] = jnp.zeros_like(inner)
        lse[...] = jnp.zeros_like(lse)

    choose(core_ref, k1, kd, kc)
    choose(core_ref, v1, vd, vc)
    query = q[...]
    scores = [dot_nt(k[...], query) * SCALE2 + bias[b] for b, k in enumerate((k0, k1, k2))]
    top = functools.reduce(jnp.maximum, [jnp.max(s, axis=0, keepdims=True) for s in scores])
    grown = [jnp.exp2(s - top) for s in scores]
    total = sum(jnp.sum(g, axis=0, keepdims=True) for g in grown)
    over = 1.0 / total
    lse[pl.ds(h, 1), :] = top + jnp.log2(total)
    out = 0.0
    for g, v in zip(grown, (v0, v1, v2)):
        out = out + dot_nn(v[...].T, (g * over).astype(BF16))
    squares[...] += out * out
    out = out.T
    o[...] = out
    inner[...] += cot[...].astype(F32) * gain[...] * out

    @pl.when(h == pl.num_programs(0) - 1)
    def _():
        stat[...] = jnp.zeros_like(stat)
        stat[0:1, :] = jnp.sum(squares[...], axis=0, keepdims=True)
        stat[1:2, :] = jnp.sum(inner[...].T, axis=0, keepdims=True)


def three_parts(value):
    high = value.astype(BF16).astype(F32)
    middle = (value - high).astype(BF16).astype(F32)
    return high, middle, (value - high - middle).astype(BF16).astype(F32)


def norm_kernel(
    features, chunks, docs, parts, lse, o, cot, gain, normed, own_stats, *rest,
):
    pieces, (inv, coef, packed) = rest[:-3], rest[-3:]
    h = pl.program_id(0)

    @pl.when(h == 0)
    def _():
        stat = parts[0:8, :] + parts[8:16, :] + parts[16:24, :] + parts[24:32, :]
        inverse = lax.rsqrt(stat[0:1, :] / features + 1e-05)
        inv[...] = as_columns(inverse)
        coef[...] = as_columns(inverse * inverse * inverse * stat[1:2, :] / features)
        own_stats[...] = jnp.zeros_like(own_stats)
        own_stats[0:16, :] = lse[...]
        own_stats[28:29, :] = docs[0:1, :]

    attended = o[...]
    normed[...] = (attended * inv[...] * gain[...]).astype(BF16)
    out = (inv[...] * (cot[...].astype(F32) * gain[...]) - attended * coef[...]).astype(BF16)
    own_stats[pl.ds(16 + h, 1), :] = jnp.sum((out.astype(F32) * attended).T, axis=0, keepdims=True)
    for piece, (first, end) in zip(pieces, chunks):

        @pl.when((h >= first) & (h < end))
        def _(piece=piece, first=first):
            if first == 0:
                piece[:, pl.ds(pl.multiple_of(h * HS, HS), HS)] = out
            else:
                piece[...] = out

    @pl.when(h == pl.num_programs(0) - 1)
    def _():
        packed[...] = jnp.zeros_like(packed)
        for i, value in enumerate(three_parts(own_stats[...])):
            packed[i * STATS : (i + 1) * STATS, :] = value
        pieces[0][:, chunks[0][1] * HS :] = packed[...].T.astype(BF16)


def own_kernel(
    chunks, core_ref, d0, d1, d2, stats, q, k0, kc, kd, k2, v0, vc, vd, v2, *rest,
):
    pieces, (dq, dk, dv, bias, k1, v1, grad) = rest[:-7], rest[-7:]
    h = pl.program_id(0)

    @pl.when(h == 0)
    def _():
        rows = [d[0:1, :] for d in (d0, d1, d2)]
        write_bias(bias, rows, [rows[0]] * 3, ("own", "near", "far"))

    for piece, (first, end) in zip(pieces, chunks):

        @pl.when((h >= first) & (h < end))
        def _(piece=piece):
            grad[...] = piece[...]

    choose(core_ref, k1, kd, kc)
    choose(core_ref, v1, vd, vc)
    query, out_grad = q[...], grad[...]
    lse = stats[pl.ds(h, 1), :]
    delta = stats[pl.ds(16 + h, 1), :]
    total = 0.0
    for b, (k, v) in enumerate(((k0, v0), (k1, v1), (k2, v2))):
        key = k[...]
        weights = jnp.exp2(dot_nt(key, query) * SCALE2 + bias[b] - lse)
        dscore = (weights * (dot_nt(v[...], out_grad) - delta)).astype(BF16)
        total = total + dot_nn(key.T, dscore)
        if b == 0:
            dk[...] = dot_nn(dscore, query)
            dv[...] = dot_nn(weights.astype(BF16), out_grad)
    dq[...] = (total.T * SCALE).astype(BF16)


def keys_kernel(
    base, aliased, core_ref, docs, pc, pd, p2, k, v, qc, qd, q2, gc, gd, g2, dk0, dv0, *rest,
):
    if aliased:
        rest = rest[2:]
    dk, dv, bias, q1, g1, packed, s1, s2 = rest
    h = pl.program_id(0)

    @pl.when(h == 0)
    def _():
        choose(core_ref, packed, pc, pd)
        for s, p in ((s1, packed), (s2, p2)):
            parts = p[...].astype(F32).T
            s[...] = parts[:STATS] + parts[STATS : 2 * STATS] + parts[2 * STATS : 3 * STATS]
        rows = [s1[28:29, :], s2[28:29, :]]
        write_bias(bias, [docs[0:1, :]] * 2, rows, ("near", "far"))

    choose(core_ref, q1, qc, qd)
    choose(core_ref, g1, gc, gd)
    key, value = k[...], v[...]
    grad_key, grad_value = dk0[...], dv0[...]
    for b, (q, g, stats) in enumerate(((q1, g1, s1), (q2, g2, s2))):
        query, out_grad = q[...], g[...]
        lse = stats[pl.ds(base + h, 1), :]
        delta = stats[pl.ds(16 + base + h, 1), :]
        weights = jnp.exp2(dot_nt(key, query) * SCALE2 + bias[b] - lse)
        dscore = (weights * (dot_nt(value, out_grad) - delta)).astype(BF16)
        grad_key = grad_key + dot_nn(dscore, query)
        grad_value = grad_value + dot_nn(weights.astype(BF16), out_grad)
    dk[...] = (grad_key * SCALE).astype(BF16)
    dv[...] = grad_value.astype(BF16)


def params():
    return dict(
        compiler_params=pltpu.CompilerParams(
            dimension_semantics=("arbitrary",), vmem_limit_bytes=60 * 1024 * 1024
        ),
        cost_estimate=pl.CostEstimate(flops=0, bytes_accessed=0, transcendentals=0),
    )


def body(queries, keys, values, cotangent, doc_ids, gain):
    rows, width = queries.shape
    heads = width // HS
    count = lax.axis_size("section")
    features = width * lax.axis_size("tp")
    section = lax.axis_index("section")
    core = lax.rem(section, 2).astype(jnp.int32).reshape(1)
    ahead = {d: [(s, s + d) for s in range(count) if 0 <= s + d < count] for d in (1, 2, -2)}
    to_core1 = [(s, s + 1) for s in range(0, count, 2)]
    to_core0 = [(s + 1, s) for s in range(0, count, 2)]
    gain = gain.reshape(1, width)

    d0 = jnp.broadcast_to((doc_ids + 1).astype(F32)[None], (8, rows))

    k2 = send(keys, ahead[2])
    v2 = send(values, ahead[2])
    d1 = send(d0, ahead[1])
    d2 = send(d0, ahead[2])
    kc = send(keys, to_core1)
    vc = send(values, to_core1)
    qc = send(queries, to_core0)
    k2, kc, vc, qc, gain = lax.optimization_barrier((k2, kc, vc, qc, gain))
    kd = send(k2, to_core0)
    chunks = [(sum(CHUNKS[:i]), sum(CHUNKS[: i + 1])) for i in range(len(CHUNKS))]
    q_first, q_last = [queries[:, a * HS : b * HS] for a, b in chunks]
    v2, d1, d2, kd, q_first, q_last = lax.optimization_barrier((v2, d1, d2, kd, q_first, q_last))

    q2a = send(q_first, ahead[-2])
    vd = send(v2, to_core0)

    smem = pl.BlockSpec(memory_space=pltpu.SMEM)

    def whole(shape):
        return pl.BlockSpec(shape, lambda h: (0, 0))

    def head(base=0):
        return pl.BlockSpec((rows, HS), lambda h: (0, base + h))

    def part(first, end):
        return pl.BlockSpec((rows, HS), lambda h: (0, jnp.clip(h, first, end - 1) - first))

    def stats_block(at):
        return pl.BlockSpec((rows, HS), lambda h: (0, at))

    def gain_head():
        return pl.BlockSpec((1, HS), lambda h: (0, h))

    tile = pltpu.VMEM((rows, HS), BF16)
    wide = jax.ShapeDtypeStruct((rows, width), F32)
    thin = jax.ShapeDtypeStruct((rows, width), BF16)
    attended, lse, stat = pl.pallas_call(
        forward_kernel,
        grid=(heads,),
        in_specs=[smem] + [whole((8, rows))] * 3 + [head()] * 10 + [gain_head()],
        out_specs=[head(), whole((16, rows)), whole((8, rows))],
        out_shape=[
            wide,
            jax.ShapeDtypeStruct((16, rows), F32),
            jax.ShapeDtypeStruct((8, rows), F32),
        ],
        scratch_shapes=[
            pltpu.VMEM((3, rows, rows), F32),
            tile,
            tile,
            pltpu.VMEM((HS, rows), F32),
            pltpu.VMEM((rows, HS), F32),
        ],
        name="forward",
        **params(),
    )(core, d0, d1, d2, queries, keys, kc, kd, k2, values, vc, vd, v2, cotangent, gain)

    parts = lax.all_gather(after(stat, q2a), "tp", tiled=True)
    q_last = after(q_last, parts)
    q2b = send(q_last, ahead[-2])

    widths = [(b - a) * HS for a, b in chunks]
    widths[0] += HS
    normed, stats, *pieces = pl.pallas_call(
        functools.partial(norm_kernel, features, chunks),
        grid=(heads,),
        in_specs=[whole((8, rows)), whole((32, rows)), whole((16, rows))]
        + [head(), head(), gain_head()],
        out_specs=[head(), whole((STATS, rows)), whole((rows, widths[0]))]
        + [part(*chunk) for chunk in chunks[1:]],
        out_shape=[thin, jax.ShapeDtypeStruct((STATS, rows), F32)]
        + [jax.ShapeDtypeStruct((rows, w), BF16) for w in widths],
        scratch_shapes=[pltpu.VMEM((rows, HS), F32)] * 2 + [pltpu.VMEM((HS, rows), F32)],
        name="norm",
        **params(),
    )(d0, parts, lse, attended, cotangent, gain)

    g2s = [send(piece, ahead[-2]) for piece in pieces]
    gcs = [send(piece, to_core0) for piece in pieces]

    grad_query, dk0, dv0 = pl.pallas_call(
        functools.partial(own_kernel, chunks),
        grid=(heads,),
        in_specs=[smem]
        + [whole((8, rows))] * 3
        + [whole((STATS, rows))]
        + [head()] * 9
        + [part(*chunk) for chunk in chunks],
        out_specs=[head()] * 3,
        out_shape=[thin, wide, wide],
        scratch_shapes=[pltpu.VMEM((3, rows, rows), F32), tile, tile, tile],
        name="own",
        **params(),
    )(core, d0, d1, d2, stats, queries, keys, kc, kd, k2, values, vc, vd, v2, *pieces)

    q2s = [q2a, q2b]
    qds = [send(q, to_core1) for q in lax.optimization_barrier((q2a, q2b, grad_query))[:2]]
    first = after(g2s[0], *qds)
    out = ()
    for a, b in HANDED:
        i = 0 if b <= CHUNKS[0] else 1
        start = a - chunks[i][0]
        if i == 0:
            end = b if b < CHUNKS[0] else b + 1
            gd = send(first[:, a * HS : end * HS], to_core1)
            if b == CHUNKS[0]:
                stats_at = b - a
                pd = gd
        else:
            gd = send(after(g2s[1], *out), to_core1)
        if a == 0:
            waiting = gd
            continue
        steps = [(a, b, gd)]
        if i == 0:
            steps = [(0, a, waiting), (a, b, gd)]
        for a, b, gd in steps:
            start = a - chunks[i][0]
            out = pl.pallas_call(
                functools.partial(keys_kernel, a, len(out) > 0),
                grid=(b - a,),
                in_specs=[smem, whole((8, rows))]
                + [stats_block(CHUNKS[0]), stats_block(stats_at), stats_block(CHUNKS[0])]
                + [head(a)] * 3
                + [head(start)] * 3
                + [head(), head(start)]
                + [head(a)] * 2
                + [pl.BlockSpec(memory_space=pl.ANY)] * len(out),
                out_specs=[head(a)] * 2,
                out_shape=[thin, thin],
                input_output_aliases={15: 0, 16: 1} if out else {},
                scratch_shapes=[pltpu.VMEM((2, rows, rows), F32), tile, tile, tile]
                + [pltpu.VMEM((STATS, rows), F32)] * 2,
                name="keys",
                **params(),
            )(
                core, d0, gcs[0], pd, g2s[0], keys, values, qc, qds[i], q2s[i],
                gcs[i], gd, g2s[i], dk0, dv0, *out,
            )
    return normed, grad_query, out[0], out[1]


def solution(mesh):
    split = P("section", "tp")
    return jax.shard_map(
        body,
        mesh=mesh,
        in_specs=(split, split, split, split, P("section"), P("tp")),
        out_specs=(split, split, split, split),
        check_vma=False,
    )
```

```python
import functools
import math

import jax
import jax.numpy as jnp
from jax import lax
from jax.experimental import pallas as pl
from jax.experimental.pallas import tpu as pltpu
from jax.sharding import PartitionSpec as P

HS = 128
SCALE = HS**-0.5
SCALE2 = SCALE * math.log2(math.e)
HIDDEN = -1e30
CHUNKS = (6, 6)
HANDED = ((0, 2), (2, 4), (4, 6))
QUERIES = 5
STATS = 32
F32 = jnp.float32
BF16 = jnp.bfloat16


def send(value, pairs):
    return lax.ppermute(value, "section", pairs)


def after(value, *earlier):
    return lax.optimization_barrier((value, *earlier))[0]


def dot_nt(a, b):
    return lax.dot_general(a, b, (((1,), (1,)), ((), ())), preferred_element_type=F32)


def dot_nn(a, b):
    return lax.dot_general(a, b, (((1,), (0,)), ((), ())), preferred_element_type=F32)


def as_columns(row):
    return jnp.broadcast_to(row, (128, row.shape[1])).T


def write_bias(bias, key_rows, query_rows, kinds):
    for b, (key_row, query_row, kind) in enumerate(zip(key_rows, query_rows, kinds)):
        n = key_row.shape[1]
        key_doc = jnp.concatenate([as_columns(key_row)] * (n // 128), axis=1)
        visible = key_doc == query_row
        key_pos = lax.broadcasted_iota(jnp.int32, (n, n), 0)
        query_pos = lax.broadcasted_iota(jnp.int32, (n, n), 1)
        if kind == "own":
            visible = visible & (key_pos <= query_pos)
        elif kind == "far":
            visible = visible & (key_pos > query_pos)
        bias[b] = jnp.where(visible, 0.0, HIDDEN)


def choose(core_ref, scratch, for_core0, for_core1):
    @pl.when(core_ref[0] == 0)
    def _():
        scratch[...] = for_core0[...]

    @pl.when(core_ref[0] != 0)
    def _():
        scratch[...] = for_core1[...]


def pick(scratch, refs, ranges, head, wanted):
    for ref, (first, end) in zip(refs, ranges):

        @pl.when(wanted & (head >= first) & (head < end))
        def _(ref=ref):
            scratch[...] = ref[...]


def forward_kernel(
    core_ref, d0, d1, d2, q, k0, kc, kd, k2, v0, vc, vd, v2, cot, gain,
    o, lse, stat, bias, k1, v1, squares, inner,
):
    h = pl.program_id(0)

    @pl.when(h == 0)
    def _():
        near = jnp.where(core_ref[0] == 0, d2[8:9, :], d1[0:1, :])
        rows = [d0[0:1, :], near, d2[0:1, :]]
        write_bias(bias, rows, [rows[0]] * 3, ("own", "near", "far"))
        squares[...] = jnp.zeros_like(squares)
        inner[...] = jnp.zeros_like(inner)
        lse[...] = jnp.zeros_like(lse)

    choose(core_ref, k1, kd, kc)
    choose(core_ref, v1, vd, vc)
    query = q[...]
    scores = [dot_nt(k[...], query) * SCALE2 + bias[b] for b, k in enumerate((k0, k1, k2))]
    top = functools.reduce(jnp.maximum, [jnp.max(s, axis=0, keepdims=True) for s in scores])
    grown = [jnp.exp2(s - top) for s in scores]
    total = sum(jnp.sum(g, axis=0, keepdims=True) for g in grown)
    over = 1.0 / total
    lse[pl.ds(h, 1), :] = top + jnp.log2(total)
    out = 0.0
    for g, v in zip(grown, (v0, v1, v2)):
        out = out + dot_nn(v[...].T, (g * over).astype(BF16))
    squares[...] += out * out
    out = out.T
    o[...] = out
    inner[...] += cot[...].astype(F32) * gain[...] * out

    @pl.when(h == pl.num_programs(0) - 1)
    def _():
        stat[...] = jnp.zeros_like(stat)
        stat[0:1, :] = jnp.sum(squares[...], axis=0, keepdims=True)
        stat[1:2, :] = jnp.sum(inner[...].T, axis=0, keepdims=True)


def three_parts(value):
    high = value.astype(BF16).astype(F32)
    middle = (value - high).astype(BF16).astype(F32)
    return high, middle, (value - high - middle).astype(BF16).astype(F32)


def norm_kernel(features, chunks, count, docs, lse, o, cot, gain, *rest):
    parts, (normed, own_stats, *rest) = rest[:count], rest[count:]
    pieces, (inv, coef, packed) = rest[:-3], rest[-3:]
    h = pl.program_id(0)

    @pl.when(h == 0)
    def _():
        stat = functools.reduce(jnp.add, [part[...] for part in parts])
        inverse = lax.rsqrt(stat[0:1, :] / features + 1e-05)
        inv[...] = as_columns(inverse)
        coef[...] = as_columns(inverse * inverse * inverse * stat[1:2, :] / features)
        own_stats[...] = jnp.zeros_like(own_stats)
        own_stats[0:16, :] = lse[...]
        own_stats[28:29, :] = docs[0:1, :]

    attended = o[...]
    normed[...] = (attended * inv[...] * gain[...]).astype(BF16)
    out = (inv[...] * (cot[...].astype(F32) * gain[...]) - attended * coef[...]).astype(BF16)
    own_stats[pl.ds(16 + h, 1), :] = jnp.sum((out.astype(F32) * attended).T, axis=0, keepdims=True)
    for piece, (first, end) in zip(pieces, chunks):

        @pl.when((h >= first) & (h < end))
        def _(piece=piece, first=first):
            if first == 0:
                piece[:, pl.ds(pl.multiple_of(h * HS, HS), HS)] = out
            else:
                piece[...] = out

    @pl.when(h == pl.num_programs(0) - 1)
    def _():
        packed[...] = jnp.zeros_like(packed)
        for i, value in enumerate(three_parts(own_stats[...])):
            packed[i * STATS : (i + 1) * STATS, :] = value
        pieces[0][:, chunks[0][1] * HS :] = packed[...].T.astype(BF16)


def own_kernel(
    chunks, core_ref, d0, d1, d2, stats, q, k0, kc, kd, k2, v0, vc, vd, v2, *rest,
):
    pieces, (dq, dk, dv, bias, k1, v1, grad) = rest[:-7], rest[-7:]
    h = pl.program_id(0)

    @pl.when(h == 0)
    def _():
        near = jnp.where(core_ref[0] == 0, d2[8:9, :], d1[0:1, :])
        rows = [d0[0:1, :], near, d2[0:1, :]]
        write_bias(bias, rows, [rows[0]] * 3, ("own", "near", "far"))

    for piece, (first, end) in zip(pieces, chunks):

        @pl.when((h >= first) & (h < end))
        def _(piece=piece):
            grad[...] = piece[...]

    choose(core_ref, k1, kd, kc)
    choose(core_ref, v1, vd, vc)
    query, out_grad = q[...], grad[...]
    lse = stats[pl.ds(h, 1), :]
    delta = stats[pl.ds(16 + h, 1), :]
    total = 0.0
    for b, (k, v) in enumerate(((k0, v0), (k1, v1), (k2, v2))):
        key = k[...]
        weights = jnp.exp2(dot_nt(key, query) * SCALE2 + bias[b] - lse)
        dscore = (weights * (dot_nt(v[...], out_grad) - delta)).astype(BF16)
        total = total + dot_nn(key.T, dscore)
        if b == 0:
            dk[...] = dot_nn(dscore, query)
            dv[...] = dot_nn(weights.astype(BF16), out_grad)
    dq[...] = (total.T * SCALE).astype(BF16)


def keys_kernel(base, q_ranges, g_ranges, core_ref, *refs):
    refs = list(refs)

    def take(n):
        taken = refs[:n]
        del refs[:n]
        return taken

    later = base > 0
    h = pl.program_id(0)
    if later:
        bias, s1, s2 = take(3)
    else:
        docs, pc, pd, p2 = take(4)
    k, v, qc = take(3)
    qds, q2s = take(len(q_ranges)), take(len(q_ranges))
    gc, g2 = take(2)
    gds = take(len(g_ranges))
    dk0, dv0 = take(2)
    if later:
        take(2)
    dk, dv = take(2)
    if not later:
        bias, s1, s2 = take(3)
    q1, q2, g1, packed = refs

    if not later:

        @pl.when(h == 0)
        def _():
            choose(core_ref, packed, pc, pd)
            for s, p in ((s1, packed), (s2, p2)):
                parts = p[...].astype(F32).T
                s[...] = parts[:STATS] + parts[STATS : 2 * STATS] + parts[2 * STATS : 3 * STATS]
            rows = [s1[28:29, :], s2[28:29, :]]
            write_bias(bias, [docs[0:1, :]] * 2, rows, ("near", "far"))

    head = base + h
    core0 = core_ref[0] == 0
    pick(q2, q2s, q_ranges, head, True)
    pick(q1, qds, q_ranges, head, core_ref[0] != 0)
    pick(q1, [qc], [(0, head + 1)], head, core0)
    pick(g1, gds, g_ranges, head, core_ref[0] != 0)
    pick(g1, [gc], [(0, head + 1)], head, core0)
    key, value = k[...], v[...]
    grad_key, grad_value = dk0[...], dv0[...]
    for b, (q, g, stats) in enumerate(((q1, g1, s1), (q2, g2, s2))):
        query, out_grad = q[...], g[...]
        lse = stats[pl.ds(head, 1), :]
        delta = stats[pl.ds(16 + head, 1), :]
        weights = jnp.exp2(dot_nt(key, query) * SCALE2 + bias[b] - lse)
        dscore = (weights * (dot_nt(value, out_grad) - delta)).astype(BF16)
        grad_key = grad_key + dot_nn(dscore, query)
        grad_value = grad_value + dot_nn(weights.astype(BF16), out_grad)
    dk[...] = (grad_key * SCALE).astype(BF16)
    dv[...] = grad_value.astype(BF16)


def params():
    return dict(
        compiler_params=pltpu.CompilerParams(
            dimension_semantics=("arbitrary",), vmem_limit_bytes=60 * 1024 * 1024
        ),
        cost_estimate=pl.CostEstimate(flops=0, bytes_accessed=0, transcendentals=0),
    )


def body(queries, keys, values, cotangent, doc_ids, gain):
    rows, width = queries.shape
    heads = width // HS
    count = lax.axis_size("section")
    features = width * lax.axis_size("tp")
    section = lax.axis_index("section")
    core = lax.rem(section, 2).astype(jnp.int32).reshape(1)
    ahead = {d: [(s, s + d) for s in range(count) if 0 <= s + d < count] for d in (2, -2)}
    to_core1 = [(s, s + 1) for s in range(0, count, 2)]
    to_core0 = [(s + 1, s) for s in range(0, count, 2)]
    gain = gain.reshape(1, width)

    d0 = jnp.broadcast_to((doc_ids + 1).astype(F32)[None], (8, rows))

    k2 = send(keys, ahead[2])
    v2 = send(values, ahead[2])
    d1 = send(d0, to_core1 + to_core0)
    d2 = send(jnp.concatenate([d0, d1], axis=0), ahead[2])
    k2, *local = lax.optimization_barrier((k2, keys, values, queries))
    kd = send(k2, to_core0)
    kc = send(local[0], to_core1)
    vc = send(local[1], to_core1)
    qc = send(local[2], to_core0)
    chunks = [(sum(CHUNKS[:i]), sum(CHUNKS[: i + 1])) for i in range(len(CHUNKS))]
    q_first, q_last = queries[:, : QUERIES * HS], queries[:, QUERIES * HS :]
    v2, d1, d2, kd, kc, vc, gain, q_first, q_last = lax.optimization_barrier(
        (v2, d1, d2, kd, kc, vc, gain, q_first, q_last)
    )

    q2a = send(q_first, ahead[-2])
    vd = send(v2, to_core0)

    smem = pl.BlockSpec(memory_space=pltpu.SMEM)

    def whole(shape):
        return pl.BlockSpec(shape, lambda h: (0, 0))

    def head(base=0):
        return pl.BlockSpec((rows, HS), lambda h: (0, base + h))

    def part(first, end):
        return pl.BlockSpec((rows, HS), lambda h: (0, jnp.clip(h, first, end - 1) - first))

    def stats_block(at):
        return pl.BlockSpec((rows, HS), lambda h: (0, at))

    def gain_head():
        return pl.BlockSpec((1, HS), lambda h: (0, h))

    tile = pltpu.VMEM((rows, HS), BF16)
    wide = jax.ShapeDtypeStruct((rows, width), F32)
    thin = jax.ShapeDtypeStruct((rows, width), BF16)
    attended, lse, stat = pl.pallas_call(
        forward_kernel,
        grid=(heads,),
        in_specs=[smem] + [whole((8, rows))] * 2 + [whole((16, rows))] + [head()] * 10 + [gain_head()],
        out_specs=[head(), whole((16, rows)), whole((8, rows))],
        out_shape=[
            wide,
            jax.ShapeDtypeStruct((16, rows), F32),
            jax.ShapeDtypeStruct((8, rows), F32),
        ],
        scratch_shapes=[
            pltpu.VMEM((3, rows, rows), F32),
            tile,
            tile,
            pltpu.VMEM((HS, rows), F32),
            pltpu.VMEM((rows, HS), F32),
        ],
        name="forward",
        **params(),
    )(core, d0, d1, d2, queries, keys, kc, kd, k2, values, vc, vd, v2, cotangent, gain)

    stat = after(stat, q2a)
    tp = lax.axis_size("tp")
    parts = [stat]
    for step in range(1, tp):
        parts.append(lax.ppermute(stat, "tp", [(i, (i + step) % tp) for i in range(tp)]))
    q_last, *parts = lax.optimization_barrier((q_last, *parts))
    q2b = send(q_last, ahead[-2])

    widths = [(b - a) * HS for a, b in chunks]
    widths[0] += HS
    normed, stats, *pieces = pl.pallas_call(
        functools.partial(norm_kernel, features, chunks, tp),
        grid=(heads,),
        in_specs=[whole((8, rows)), whole((16, rows)), head(), head(), gain_head()]
        + [whole((8, rows))] * tp,
        out_specs=[head(), whole((STATS, rows)), whole((rows, widths[0]))]
        + [part(*chunk) for chunk in chunks[1:]],
        out_shape=[thin, jax.ShapeDtypeStruct((STATS, rows), F32)]
        + [jax.ShapeDtypeStruct((rows, w), BF16) for w in widths],
        scratch_shapes=[pltpu.VMEM((rows, HS), F32)] * 2 + [pltpu.VMEM((HS, rows), F32)],
        name="norm",
        **params(),
    )(d0, lse, attended, cotangent, gain, *parts)

    g2s = [send(piece, ahead[-2]) for piece in pieces]
    gcs = [send(piece, to_core0) for piece in pieces]

    grad_query, dk0, dv0 = pl.pallas_call(
        functools.partial(own_kernel, chunks),
        grid=(heads,),
        in_specs=[smem]
        + [whole((8, rows))] * 2
        + [whole((16, rows)), whole((STATS, rows))]
        + [head()] * 9
        + [part(*chunk) for chunk in chunks],
        out_specs=[head()] * 3,
        out_shape=[thin, wide, wide],
        scratch_shapes=[pltpu.VMEM((3, rows, rows), F32), tile, tile, tile],
        name="own",
        **params(),
    )(core, d0, d1, d2, stats, queries, keys, kc, kd, k2, values, vc, vd, v2, *pieces)

    q2s = [q2a, q2b]
    qds = [send(q, to_core1) for q in lax.optimization_barrier((q2a, q2b, grad_query))[:2]]
    first = after(g2s[0], *qds)
    middle = CHUNKS[0]
    gds = []
    for a, b in HANDED:
        gds.append(send(first[:, a * HS : (b if b < middle else b + 1) * HS], to_core1))

    def spread(base, ranges):
        return [
            pl.BlockSpec((rows, HS), lambda h, f=f, e=e: (0, jnp.clip(base + h, f, e - 1) - f))
            for f, e in ranges
        ]

    q_ranges = [(0, QUERIES), (QUERIES, heads)]
    both = [head()] * 2
    bias_block = pl.BlockSpec((2, rows, rows), lambda h: (0, 0, 0))
    stats_type = jax.ShapeDtypeStruct((STATS, rows), F32)
    scratch = [tile] * 4
    dk, dv, bias, s1, s2 = pl.pallas_call(
        functools.partial(keys_kernel, 0, q_ranges, HANDED),
        grid=(middle,),
        in_specs=[smem, whole((8, rows)), stats_block(middle)]
        + [stats_block(HANDED[-1][1] - HANDED[-1][0]), stats_block(middle)]
        + [head()] * 3
        + spread(0, q_ranges) * 2
        + both
        + spread(0, HANDED)
        + both,
        out_specs=both + [bias_block] + [whole((STATS, rows))] * 2,
        out_shape=[thin, thin, jax.ShapeDtypeStruct((2, rows, rows), F32)] + [stats_type] * 2,
        scratch_shapes=scratch,
        name="keys",
        **params(),
    )(
        core, d0, gcs[0], gds[-1], g2s[0], keys, values, qc, *qds, *q2s,
        gcs[0], g2s[0], *gds, dk0, dv0,
    )
    gd = send(after(g2s[1], dk), to_core1)
    rest = [(middle, heads)]
    dk, dv = pl.pallas_call(
        functools.partial(keys_kernel, middle, q_ranges[1:], rest),
        grid=(heads - middle,),
        in_specs=[smem, bias_block]
        + [whole((STATS, rows))] * 2
        + [head(middle)] * 3
        + spread(middle, q_ranges[1:]) * 2
        + both
        + spread(middle, rest)
        + [head(middle)] * 2
        + [pl.BlockSpec(memory_space=pl.ANY)] * 2,
        out_specs=[head(middle)] * 2,
        out_shape=[thin, thin],
        input_output_aliases={14: 0, 15: 1},
        scratch_shapes=scratch,
        name="keys",
        **params(),
    )(
        core, bias, s1, s2, keys, values, qc, qds[1], q2s[1],
        gcs[1], g2s[1], gd, dk0, dv0, dk, dv,
    )
    return normed, grad_query, dk, dv


def solution(mesh):
    split = P("section", "tp")
    return jax.shard_map(
        body,
        mesh=mesh,
        in_specs=(split, split, split, split, P("section"), P("tp")),
        out_specs=(split, split, split, split),
        check_vma=False,
    )
```

```python
import functools
import math

import jax
import jax.numpy as jnp
from jax import lax
from jax.experimental import pallas as pl
from jax.experimental.pallas import tpu as pltpu
from jax.sharding import PartitionSpec as P

HS = 128
SCALE = HS**-0.5
SCALE2 = SCALE * math.log2(math.e)
HIDDEN = -1e30
CHUNKS = (6, 6)
HANDED = ((0, 3), (3, 6))
QUERIES = 5
STATS = 32
F32 = jnp.float32
BF16 = jnp.bfloat16


def send(value, pairs):
    return lax.ppermute(value, "section", pairs)


def after(value, *earlier):
    return lax.optimization_barrier((value, *earlier))[0]


def dot_nt(a, b):
    return lax.dot_general(a, b, (((1,), (1,)), ((), ())), preferred_element_type=F32)


def dot_nn(a, b):
    return lax.dot_general(a, b, (((1,), (0,)), ((), ())), preferred_element_type=F32)


def as_columns(row):
    return jnp.broadcast_to(row, (128, row.shape[1])).T


def write_bias(bias, key_rows, query_rows, kinds):
    for b, (key_row, query_row, kind) in enumerate(zip(key_rows, query_rows, kinds)):
        n = key_row.shape[1]
        key_doc = jnp.concatenate([as_columns(key_row)] * (n // 128), axis=1)
        visible = key_doc == query_row
        key_pos = lax.broadcasted_iota(jnp.int32, (n, n), 0)
        query_pos = lax.broadcasted_iota(jnp.int32, (n, n), 1)
        if kind == "own":
            visible = visible & (key_pos <= query_pos)
        elif kind == "far":
            visible = visible & (key_pos > query_pos)
        bias[b] = jnp.where(visible, 0.0, HIDDEN)


def choose(core_ref, scratch, for_core0, for_core1):
    @pl.when(core_ref[0] == 0)
    def _():
        scratch[...] = for_core0[...]

    @pl.when(core_ref[0] != 0)
    def _():
        scratch[...] = for_core1[...]


def pick(scratch, refs, ranges, head, wanted):
    for ref, (first, end) in zip(refs, ranges):

        @pl.when(wanted & (head >= first) & (head < end))
        def _(ref=ref):
            scratch[...] = ref[...]


def forward_kernel(
    core_ref, d0, d1, d2, q, k0, kc, kd, k2, v0, vc, vd, v2, cot, gain,
    o, lse, stat, bias, k1, v1, squares, inner,
):
    h = pl.program_id(0)

    @pl.when(h == 0)
    def _():
        near = jnp.where(core_ref[0] == 0, d2[8:9, :], d1[0:1, :])
        rows = [d0[0:1, :], near, d2[0:1, :]]
        write_bias(bias, rows, [rows[0]] * 3, ("own", "near", "far"))
        squares[...] = jnp.zeros_like(squares)
        inner[...] = jnp.zeros_like(inner)
        lse[...] = jnp.zeros_like(lse)

    choose(core_ref, k1, kd, kc)
    choose(core_ref, v1, vd, vc)
    query = q[...]
    scores = [dot_nt(k[...], query) * SCALE2 + bias[b] for b, k in enumerate((k0, k1, k2))]
    top = functools.reduce(jnp.maximum, [jnp.max(s, axis=0, keepdims=True) for s in scores])
    grown = [jnp.exp2(s - top) for s in scores]
    total = sum(jnp.sum(g, axis=0, keepdims=True) for g in grown)
    over = 1.0 / total
    lse[pl.ds(h, 1), :] = top + jnp.log2(total)
    out = 0.0
    for g, v in zip(grown, (v0, v1, v2)):
        out = out + dot_nn(v[...].T, (g * over).astype(BF16))
    squares[...] += out * out
    out = out.T
    o[...] = out
    inner[...] += cot[...].astype(F32) * gain[...] * out

    @pl.when(h == pl.num_programs(0) - 1)
    def _():
        stat[...] = jnp.zeros_like(stat)
        stat[0:1, :] = jnp.sum(squares[...], axis=0, keepdims=True)
        stat[1:2, :] = jnp.sum(inner[...].T, axis=0, keepdims=True)


def three_parts(value):
    high = value.astype(BF16).astype(F32)
    middle = (value - high).astype(BF16).astype(F32)
    return high, middle, (value - high - middle).astype(BF16).astype(F32)


def norm_kernel(features, chunks, count, docs, lse, o, cot, gain, *rest):
    parts, (normed, own_stats, *rest) = rest[:count], rest[count:]
    pieces, (inv, coef, packed) = rest[:-3], rest[-3:]
    h = pl.program_id(0)

    @pl.when(h == 0)
    def _():
        stat = functools.reduce(jnp.add, [part[...] for part in parts])
        inverse = lax.rsqrt(stat[0:1, :] / features + 1e-05)
        inv[...] = as_columns(inverse)
        coef[...] = as_columns(inverse * inverse * inverse * stat[1:2, :] / features)
        own_stats[...] = jnp.zeros_like(own_stats)
        own_stats[0:16, :] = lse[...]
        own_stats[28:29, :] = docs[0:1, :]

    attended = o[...]
    normed[...] = (attended * inv[...] * gain[...]).astype(BF16)
    out = (inv[...] * (cot[...].astype(F32) * gain[...]) - attended * coef[...]).astype(BF16)
    own_stats[pl.ds(16 + h, 1), :] = jnp.sum((out.astype(F32) * attended).T, axis=0, keepdims=True)
    for piece, (first, end) in zip(pieces, chunks):

        @pl.when((h >= first) & (h < end))
        def _(piece=piece, first=first):
            if first == 0:
                piece[:, pl.ds(pl.multiple_of(h * HS, HS), HS)] = out
            else:
                piece[...] = out

    @pl.when(h == pl.num_programs(0) - 1)
    def _():
        packed[...] = jnp.zeros_like(packed)
        for i, value in enumerate(three_parts(own_stats[...])):
            packed[i * STATS : (i + 1) * STATS, :] = value
        pieces[0][:, chunks[0][1] * HS :] = packed[...].T.astype(BF16)


def own_kernel(
    chunks, core_ref, d0, d1, d2, stats, q, k0, kc, kd, k2, v0, vc, vd, v2, *rest,
):
    pieces, (dq, dk, dv, bias, k1, v1, grad) = rest[:-7], rest[-7:]
    h = pl.program_id(0)

    @pl.when(h == 0)
    def _():
        near = jnp.where(core_ref[0] == 0, d2[8:9, :], d1[0:1, :])
        rows = [d0[0:1, :], near, d2[0:1, :]]
        write_bias(bias, rows, [rows[0]] * 3, ("own", "near", "far"))

    for piece, (first, end) in zip(pieces, chunks):

        @pl.when((h >= first) & (h < end))
        def _(piece=piece):
            grad[...] = piece[...]

    choose(core_ref, k1, kd, kc)
    choose(core_ref, v1, vd, vc)
    query, out_grad = q[...], grad[...]
    lse = stats[pl.ds(h, 1), :]
    delta = stats[pl.ds(16 + h, 1), :]
    total = 0.0
    for b, (k, v) in enumerate(((k0, v0), (k1, v1), (k2, v2))):
        key = k[...]
        weights = jnp.exp2(dot_nt(key, query) * SCALE2 + bias[b] - lse)
        dscore = (weights * (dot_nt(v[...], out_grad) - delta)).astype(BF16)
        total = total + dot_nn(key.T, dscore)
        if b == 0:
            dk[...] = dot_nn(dscore, query)
            dv[...] = dot_nn(weights.astype(BF16), out_grad)
    dq[...] = (total.T * SCALE).astype(BF16)


def keys_kernel(base, q_ranges, g_ranges, core_ref, *refs):
    refs = list(refs)

    def take(n):
        taken = refs[:n]
        del refs[:n]
        return taken

    later = base > 0
    h = pl.program_id(0)
    if later:
        bias, s1, s2 = take(3)
    else:
        docs, pc, pd, p2 = take(4)
    k, v, qc = take(3)
    qds, q2s = take(len(q_ranges)), take(len(q_ranges))
    gc, g2 = take(2)
    gds = take(len(g_ranges))
    dk0, dv0 = take(2)
    if later:
        take(2)
    dk, dv = take(2)
    if not later:
        bias, s1, s2 = take(3)
    q1, q2, g1, packed = refs

    if not later:

        @pl.when(h == 0)
        def _():
            choose(core_ref, packed, pc, pd)
            for s, p in ((s1, packed), (s2, p2)):
                parts = p[...].astype(F32).T
                s[...] = parts[:STATS] + parts[STATS : 2 * STATS] + parts[2 * STATS : 3 * STATS]
            rows = [s1[28:29, :], s2[28:29, :]]
            write_bias(bias, [docs[0:1, :]] * 2, rows, ("near", "far"))

    head = base + h
    core0 = core_ref[0] == 0
    pick(q2, q2s, q_ranges, head, True)
    pick(q1, qds, q_ranges, head, core_ref[0] != 0)
    pick(q1, [qc], [(0, head + 1)], head, core0)
    pick(g1, gds, g_ranges, head, core_ref[0] != 0)
    pick(g1, [gc], [(0, head + 1)], head, core0)
    key, value = k[...], v[...]
    grad_key, grad_value = dk0[...], dv0[...]
    for b, (q, g, stats) in enumerate(((q1, g1, s1), (q2, g2, s2))):
        query, out_grad = q[...], g[...]
        lse = stats[pl.ds(head, 1), :]
        delta = stats[pl.ds(16 + head, 1), :]
        weights = jnp.exp2(dot_nt(key, query) * SCALE2 + bias[b] - lse)
        dscore = (weights * (dot_nt(value, out_grad) - delta)).astype(BF16)
        grad_key = grad_key + dot_nn(dscore, query)
        grad_value = grad_value + dot_nn(weights.astype(BF16), out_grad)
    dk[...] = (grad_key * SCALE).astype(BF16)
    dv[...] = grad_value.astype(BF16)


def params():
    return dict(
        compiler_params=pltpu.CompilerParams(
            dimension_semantics=("arbitrary",), vmem_limit_bytes=60 * 1024 * 1024
        ),
        cost_estimate=pl.CostEstimate(flops=0, bytes_accessed=0, transcendentals=0),
    )


def body(queries, keys, values, cotangent, doc_ids, gain):
    rows, width = queries.shape
    heads = width // HS
    count = lax.axis_size("section")
    features = width * lax.axis_size("tp")
    section = lax.axis_index("section")
    core = lax.rem(section, 2).astype(jnp.int32).reshape(1)
    ahead = {d: [(s, s + d) for s in range(count) if 0 <= s + d < count] for d in (2, -2)}
    to_core1 = [(s, s + 1) for s in range(0, count, 2)]
    to_core0 = [(s + 1, s) for s in range(0, count, 2)]
    gain = gain.reshape(1, width)

    d0 = jnp.broadcast_to((doc_ids + 1).astype(F32)[None], (8, rows))

    k2 = send(keys, ahead[2])
    v2 = send(values, ahead[2])
    d1 = send(d0, to_core1 + to_core0)
    d2 = send(jnp.concatenate([d0, d1], axis=0), ahead[2])
    k2, *local = lax.optimization_barrier((k2, keys, values, queries))
    kd = send(k2, to_core0)
    kc = send(local[0], to_core1)
    vc = send(local[1], to_core1)
    qc = send(local[2], to_core0)
    chunks = [(sum(CHUNKS[:i]), sum(CHUNKS[: i + 1])) for i in range(len(CHUNKS))]
    q_first, q_last = queries[:, : QUERIES * HS], queries[:, QUERIES * HS :]
    v2, d1, d2, kd, kc, vc, qc, gain, q_first, q_last = lax.optimization_barrier(
        (v2, d1, d2, kd, kc, vc, qc, gain, q_first, q_last)
    )

    q2a = send(q_first, ahead[-2])
    vd = send(v2, to_core0)

    smem = pl.BlockSpec(memory_space=pltpu.SMEM)

    def whole(shape):
        return pl.BlockSpec(shape, lambda h: (0, 0))

    def head(base=0):
        return pl.BlockSpec((rows, HS), lambda h: (0, base + h))

    def part(first, end):
        return pl.BlockSpec((rows, HS), lambda h: (0, jnp.clip(h, first, end - 1) - first))

    def stats_block(at):
        return pl.BlockSpec((rows, HS), lambda h: (0, at))

    def gain_head():
        return pl.BlockSpec((1, HS), lambda h: (0, h))

    tile = pltpu.VMEM((rows, HS), BF16)
    wide = jax.ShapeDtypeStruct((rows, width), F32)
    thin = jax.ShapeDtypeStruct((rows, width), BF16)
    attended, lse, stat = pl.pallas_call(
        forward_kernel,
        grid=(heads,),
        in_specs=[smem] + [whole((8, rows))] * 2 + [whole((16, rows))] + [head()] * 10 + [gain_head()],
        out_specs=[head(), whole((16, rows)), whole((8, rows))],
        out_shape=[
            wide,
            jax.ShapeDtypeStruct((16, rows), F32),
            jax.ShapeDtypeStruct((8, rows), F32),
        ],
        scratch_shapes=[
            pltpu.VMEM((3, rows, rows), F32),
            tile,
            tile,
            pltpu.VMEM((HS, rows), F32),
            pltpu.VMEM((rows, HS), F32),
        ],
        name="forward",
        **params(),
    )(core, d0, d1, d2, queries, keys, kc, kd, k2, values, vc, vd, v2, cotangent, gain)

    stat = after(stat, q2a)
    tp = lax.axis_size("tp")
    parts = [stat]
    for step in range(1, tp):
        parts.append(lax.ppermute(stat, "tp", [(i, (i + step) % tp) for i in range(tp)]))
    q_last, *parts = lax.optimization_barrier((q_last, *parts))
    q2b = send(q_last, ahead[-2])

    widths = [(b - a) * HS for a, b in chunks]
    widths[0] += HS
    normed, stats, *pieces = pl.pallas_call(
        functools.partial(norm_kernel, features, chunks, tp),
        grid=(heads,),
        in_specs=[whole((8, rows)), whole((16, rows)), head(), head(), gain_head()]
        + [whole((8, rows))] * tp,
        out_specs=[head(), whole((STATS, rows)), whole((rows, widths[0]))]
        + [part(*chunk) for chunk in chunks[1:]],
        out_shape=[thin, jax.ShapeDtypeStruct((STATS, rows), F32)]
        + [jax.ShapeDtypeStruct((rows, w), BF16) for w in widths],
        scratch_shapes=[pltpu.VMEM((rows, HS), F32)] * 2 + [pltpu.VMEM((HS, rows), F32)],
        name="norm",
        **params(),
    )(d0, lse, attended, cotangent, gain, *parts)

    g2s = [send(piece, ahead[-2]) for piece in pieces]
    gcs = [send(piece, to_core0) for piece in pieces]

    grad_query, dk0, dv0 = pl.pallas_call(
        functools.partial(own_kernel, chunks),
        grid=(heads,),
        in_specs=[smem]
        + [whole((8, rows))] * 2
        + [whole((16, rows)), whole((STATS, rows))]
        + [head()] * 9
        + [part(*chunk) for chunk in chunks],
        out_specs=[head()] * 3,
        out_shape=[thin, wide, wide],
        scratch_shapes=[pltpu.VMEM((3, rows, rows), F32), tile, tile, tile],
        name="own",
        **params(),
    )(core, d0, d1, d2, stats, queries, keys, kc, kd, k2, values, vc, vd, v2, *pieces)

    q2s = [q2a, q2b]
    qds = [send(q, to_core1) for q in lax.optimization_barrier((q2a, q2b, grad_query))[:2]]
    first = after(g2s[0], *qds)
    middle = CHUNKS[0]
    gds = []
    for a, b in HANDED:
        gds.append(send(first[:, a * HS : (b if b < middle else b + 1) * HS], to_core1))

    def spread(base, ranges):
        return [
            pl.BlockSpec((rows, HS), lambda h, f=f, e=e: (0, jnp.clip(base + h, f, e - 1) - f))
            for f, e in ranges
        ]

    q_ranges = [(0, QUERIES), (QUERIES, heads)]
    both = [head()] * 2
    bias_block = pl.BlockSpec((2, rows, rows), lambda h: (0, 0, 0))
    stats_type = jax.ShapeDtypeStruct((STATS, rows), F32)
    scratch = [tile] * 4
    dk, dv, bias, s1, s2 = pl.pallas_call(
        functools.partial(keys_kernel, 0, q_ranges, HANDED),
        grid=(middle,),
        in_specs=[smem, whole((8, rows)), stats_block(middle)]
        + [stats_block(HANDED[-1][1] - HANDED[-1][0]), stats_block(middle)]
        + [head()] * 3
        + spread(0, q_ranges) * 2
        + both
        + spread(0, HANDED)
        + both,
        out_specs=both + [bias_block] + [whole((STATS, rows))] * 2,
        out_shape=[thin, thin, jax.ShapeDtypeStruct((2, rows, rows), F32)] + [stats_type] * 2,
        scratch_shapes=scratch,
        name="keys",
        **params(),
    )(
        core, d0, gcs[0], gds[-1], g2s[0], keys, values, qc, *qds, *q2s,
        gcs[0], g2s[0], *gds, dk0, dv0,
    )
    gd = send(after(g2s[1], dk), to_core1)
    rest = [(middle, heads)]
    dk, dv = pl.pallas_call(
        functools.partial(keys_kernel, middle, q_ranges[1:], rest),
        grid=(heads - middle,),
        in_specs=[smem, bias_block]
        + [whole((STATS, rows))] * 2
        + [head(middle)] * 3
        + spread(middle, q_ranges[1:]) * 2
        + both
        + spread(middle, rest)
        + [head(middle)] * 2
        + [pl.BlockSpec(memory_space=pl.ANY)] * 2,
        out_specs=[head(middle)] * 2,
        out_shape=[thin, thin],
        input_output_aliases={14: 0, 15: 1},
        scratch_shapes=scratch,
        name="keys",
        **params(),
    )(
        core, bias, s1, s2, keys, values, qc, qds[1], q2s[1],
        gcs[1], g2s[1], gd, dk0, dv0, dk, dv,
    )
    return normed, grad_query, dk, dv


def solution(mesh):
    split = P("section", "tp")
    return jax.shard_map(
        body,
        mesh=mesh,
        in_specs=(split, split, split, split, P("section"), P("tp")),
        out_specs=(split, split, split, split),
        check_vma=False,
    )
```
